256 devices in a mesh: dp: 4 (over x), ctx: 16 (over z, core), exp: 4 (over y).
Axes of the slice: x: 4, y: 4, z: 8, core: 2. Of those that a mesh axis runs over, the one named last changes fastest.
Arguments:
- d_out: bfloat16 [4, 8192, 5120], P('dp', ('ctx', 'exp')), may hold values from -3 to 3
- route_ids: int32 [4, 8192, 6], P('dp', ('ctx', 'exp')), may hold values from 0 to 63, all different within a row; in each aligned block of 128 rows (0 to 127, 128 to 255, ..., all dimensions but the last counted through in order) at most 14 rows name the same one
- gate_weights: float32 [4, 8192, 6], P('dp', ('ctx', 'exp')), may hold values from 0.1 to 2
- saved_hidden: bfloat16 [4, 64, 896, 768], P('dp', ('ctx', 'exp')), may hold values from -6 to 6
- down_weight: bfloat16 [64, 5120, 768], P(('ctx', 'exp'), 'dp'), may hold values from -0.21875 to 0.21875
Outputs:
- d_hidden: bfloat16 [4, 64, 896, 768], P('dp', ('ctx', 'exp'))
- weight_grad: float32 [64, 5120, 768], P(('ctx', 'exp'), 'dp')
The draws below stay inside these ranges and needn't reach their ends.
Inputs may be any that keep to these rules, and one draw needn't show every extreme that they name: `route_ids`: each token names 6 different experts; within a sequence the tokens of one device (aligned blocks of 128) name no expert more than 14 times, and some block names one exactly 14 times.
All inputs are finite; a program needn't handle non-finite values.
Results may differ from the reference program's by a relative error of at most 0.0049.
Values may be sent and summed in bfloat16 or wider, within the bound.
A program may use at most 128 MiB of HBM per device.

```python
import math
import jax
import jax.numpy as jnp
import numpy as np
from jax import lax

D = 5120
F = 768
TOPK = 6
TOK_DEV = 128
SEQS = 4
SOURCES = 64
EXPERTS = 64
SEQ_LEN = 8192
CAP = 14
SLOTS = 896


def steps_of(stream_key, extent, split, least, top_value):
    def one(axis_at, parts):
        heights = jax.random.uniform(jax.random.fold_in(jax.random.fold_in(stream_key, 6), axis_at), (parts,), jnp.float32, least / len(split), top_value / len(split))
        return jnp.repeat(jnp.exp(heights), extent[axis_at] // parts).reshape((-1,) + (1,) * (len(extent) - axis_at - 1))

    gain = one(*split[0])
    for cut in split[1:]:
        gain = gain * one(*cut)
    return gain


def deal_out(own_key, own, number, rows, amount, top, bound, lean):
    order = jax.random.permutation(own_key, amount)
    crowded, ordinary = load_shares(amount, rows * top, bound, lean, True), load_shares(amount, rows * top, bound, lean, False)
    places = jnp.arange(amount)

    def named(tallies, rotation):
        used = int((tallies > 0).sum())
        fixed = max(1, used // 4)
        passed = fixed + (places - fixed + rotation * (used - fixed)) % max(1, amount - fixed)
        return jnp.zeros((amount,), jnp.int32).at[order[jnp.where(places < fixed, places, passed)]].set(jnp.asarray(tallies, jnp.int32))

    tallies = jnp.where(number % 4 == 0, named(crowded, number // 4), named(ordinary, number - number // 4 - 1))
    mixed = jax.random.permutation(jax.random.fold_in(own, 3), amount)
    source_of, receiver = mixed[0:amount // 2 * 2:2], mixed[1:amount // 2 * 2:2]
    slack = jnp.minimum(tallies[source_of] - 1, bound - tallies[receiver]) // 2
    slack = jnp.where((source_of == order[0]) | (receiver == order[0]) | (tallies[receiver] == 0), 0, jnp.maximum(slack, 0))
    passed = jax.random.randint(jax.random.fold_in(own, 4), (amount // 2,), 0, 1 << 20) % (slack + 1)
    tallies = tallies.at[source_of].add(-passed).at[receiver].add(passed)
    labels = jnp.searchsorted(jnp.cumsum(tallies), jnp.arange(rows * top), side="right").astype(jnp.int32)
    listing = labels.reshape(top, rows).T
    listing = listing[jax.random.permutation(jax.random.fold_in(own, 1), rows)]
    rotation = jax.random.randint(jax.random.fold_in(own, 2), (rows, 1), 0, top)
    return jnp.take_along_axis(listing, (jnp.arange(top)[None, :] + rotation) % top, axis=1)


def load_shares(count, total, limit, skew, full):
    weights = [(1 << 20) // math.isqrt(standing ** skew) + 1 for standing in range(1, count + 1)]
    largest = limit if full else min(limit, max(-(-total // count), total * weights[0] // sum(weights)))
    least = 1 if total - largest >= count - 1 else 0
    given, spare = [largest] + [least] * (count - 1), total - largest - least * (count - 1)
    while spare > 0:
        movable = [i for i in range(1, count) if given[i] < largest] or [i for i in range(1, count) if given[i] < limit]
        whole, left = sum([weights[i] for i in movable]), spare
        for i in movable:
            more = min(limit - given[i], max(1, left * weights[i] // whole), spare)
            given[i] = given[i] + more
            spare = spare - more
    return np.array(given)


def scatter_about(rng, extent, spread, bound, split=(), kind=jnp.bfloat16):
    values = spread * jax.random.normal(rng, extent, jnp.float32)
    if split:
        values = values * steps_of(rng, extent, split, -0.22, 0.18)
    return jnp.clip(values, -bound, bound).astype(kind)


def setup_inputs(seed: int = 0) -> dict:
    seeds = jax.random.split(jax.random.key(seed), 6)
    d_out = scatter_about(seeds[0], (SEQS, SEQ_LEN, D), 0.2, 3.0, ((0, 4), (1, 64)))
    route_ids_keys = jax.random.split(jax.random.fold_in(seeds[1], 1), SEQS * SEQ_LEN // TOK_DEV)
    route_ids_turns = jax.random.permutation(jax.random.fold_in(seeds[1], 3), SEQS * SEQ_LEN // TOK_DEV)
    route_ids = jax.vmap(lambda own, number: deal_out(jax.random.fold_in(seeds[1], 2), own, number, TOK_DEV, EXPERTS, TOPK, CAP, 2))(route_ids_keys, route_ids_turns).reshape((SEQS, SEQ_LEN, TOPK))
    gate_weights = jnp.clip(jnp.exp(math.log(2.0) - 2.9957323 * jax.random.uniform(seeds[2], (SEQS, SEQ_LEN, TOPK), jnp.float32) ** steps_of(seeds[2], (SEQS, SEQ_LEN, TOPK), ((0, 4), (1, 64)), -0.2, 0.2)), 0.1, 2.0)
    saved_hidden = scatter_about(seeds[3], (SEQS, EXPERTS, SLOTS, F), 1.0, 6.0, ((0, 4), (1, 64)))
    down_weight = scatter_about(seeds[4], (EXPERTS, D, F), F ** -0.5, 0.21875, ((0, 64), (1, 4)))
    return {"d_out": d_out, "route_ids": route_ids, "gate_weights": gate_weights, "saved_hidden": saved_hidden, "down_weight": down_weight}


def buckets(operands):
    ids_block, gates_block, grads_block = operands
    flat_ids = ids_block.reshape(-1).astype(jnp.int32)
    onehot = (flat_ids[:, None] == jnp.arange(EXPERTS, dtype=jnp.int32)[None, :]).astype(jnp.int32)
    before = jnp.cumsum(onehot, axis=0) - onehot
    position = jnp.sum(before * onehot, axis=1).astype(jnp.int32)
    target = (flat_ids * CAP + position).astype(jnp.int32)
    slot_rows = (gates_block[:, :, None] * grads_block[:, None, :].astype(jnp.float32)).astype(jnp.bfloat16).reshape(-1, D)
    return jnp.zeros((EXPERTS * CAP, D), jnp.bfloat16).at[target].set(slot_rows)


def expert_work(operands):
    slot_rows, hidden, weight = operands
    rows_wide = slot_rows.astype(jnp.float32)
    d_rows = jnp.einsum('srd,df->srf', rows_wide, weight.astype(jnp.float32))
    w_grad = jnp.einsum('srd,srf->df', rows_wide, hidden.astype(jnp.float32))
    return d_rows.astype(jnp.bfloat16), w_grad


def reference(d_out, route_ids, gate_weights, saved_hidden, down_weight):
    per_seq = []
    for sequence in range(SEQS):
        blocks = lax.map(buckets, (route_ids[sequence].reshape(SOURCES, TOK_DEV, TOPK),
                                   gate_weights[sequence].reshape(SOURCES, TOK_DEV, TOPK),
                                   d_out[sequence].reshape(SOURCES, TOK_DEV, D)))
        blocks = blocks.reshape(SOURCES, EXPERTS, CAP, D).transpose(1, 0, 2, 3).reshape(EXPERTS, SLOTS, D)
        per_seq.append(blocks)
    routed = jnp.stack(per_seq, axis=1)
    d_hidden, weight_grad = lax.map(expert_work, (routed, saved_hidden.transpose(1, 0, 2, 3), down_weight))
    return d_hidden.transpose(1, 0, 2, 3), weight_grad
```

```python
import functools

import jax
import jax.numpy as jnp
from jax import lax
from jax.experimental import pallas as pl
from jax.experimental.pallas import tpu as pltpu
from jax.sharding import PartitionSpec as P

MESH = pl.DeviceIdType.MESH
F32, BF16, I32 = jnp.float32, jnp.bfloat16, jnp.int32

NX, NY, NZ, NC = 4, 4, 8, 2
TOK, CAP, FF = 128, 14, 768
GROUPS = NY * NC
PART = NZ * CAP
SLOTS = GROUPS * PART
WIDTH = 1280
HALF = SLOTS // 2
TILE = 128

CHUNKS = (
    (0, 0, 256),
    (2, 0, 640),
    (2, 640, 640),
    (1, 0, 640),
    (1, 640, 640),
    (3, 0, 640),
    (3, 640, 640),
    (0, 256, 512),
    (0, 768, 512),
)
NK = len(CHUNKS)
COL = [sum(c[2] for c in CHUNKS[:k]) for k in range(NK)]
WMAX = max(c[2] for c in CHUNKS)
NSB = 3
HOPS = [(4, 3) if k % 2 == 0 else (3, 4) for k in range(NK)]


def kernel(
    d_out, ids_t, gate_t, hidden, weight, dh_out, wg_out,
    rows, sendbuf, routed, hid, raw, wts, acc, part, part2, partr,
    meta, plane, target,
    loc_sem, xs, xr, ms, mr, gs, gr, rs, rr, ys, yr, hs, hr, ps, pr,
):
    i = lax.axis_index("dp")
    ctx = lax.axis_index("ctx")
    y = lax.axis_index("exp")
    z = ctx // NC
    c = lax.rem(ctx, NC)

    def dev(dx=0, dz=0, dc=0, dy=0):
        return (
            lax.rem(i + dx, NX),
            lax.rem(z + dz, NZ) * NC + lax.rem(c + dc, NC),
            lax.rem(y + dy, NY),
        )

    def remote(src, dst, send, recv, to):
        return pltpu.make_async_remote_copy(
            src_ref=src, dst_ref=dst, send_sem=send, recv_sem=recv, device_id=to, device_id_type=MESH
        )

    load_hidden = pltpu.make_async_copy(hidden.at[0, 0], raw, loc_sem.at[0])
    load_hidden.start()
    load_weight = pltpu.make_async_copy(weight.at[0], wts, loc_sem.at[1])
    load_weight.start()
    own = {}
    for k, (o, first, w) in enumerate(CHUNKS):
        if o == 0:
            start = pl.multiple_of(i * WIDTH + first, 128)
            own[k] = pltpu.make_async_copy(
                d_out.at[0, :, pl.ds(start, w)], rows.at[0:TOK, COL[k] : COL[k] + w], loc_sem.at[2 + k]
            )
            own[k].start()

    barrier = pltpu.get_barrier_semaphore()
    peers = [dict(dx=a) for a in range(1, NX)] + [dict(dz=a) for a in range(1, NZ)]
    peers += [dict(dc=j // NY, dy=j % NY) for j in range(1, GROUPS)]
    for p in peers:
        pl.semaphore_signal(barrier, inc=1, device_id=dev(**p), device_id_type=MESH)

    r = lax.broadcasted_iota(I32, (NZ * GROUPS, TOK), 0)
    dz, dc, dy = r // GROUPS, (r // NY) % NC, r % NY
    expert = ((z + dz) % NZ) * GROUPS + ((c + dc) % NC) * NY + (y + dy) % NY
    gates = jnp.zeros((NZ * GROUPS, TOK), F32)
    for k in range(ids_t.shape[0]):
        gates += jnp.where(ids_t[k : k + 1, :] == expert, gate_t[k : k + 1, :], 0.0)
    meta[0] = gates.reshape(NZ, GROUPS, TOK)

    pl.semaphore_wait(barrier, len(peers))

    mcopy = {}
    for o in range(1, NX):
        mcopy[o] = remote(meta.at[0], meta.at[o], ms.at[o], mr.at[o], dev(dx=NX - o))
        mcopy[o].start()
    xcopy = {}
    for k, (o, first, w) in enumerate(CHUNKS):
        if o:
            start = pl.multiple_of(lax.rem(i + NX - o, NX) * WIDTH + first, 128)
            xcopy[k] = remote(
                d_out.at[0, :, pl.ds(start, w)], rows.at[0:TOK, COL[k] : COL[k] + w],
                xs.at[k], xr.at[k], dev(dx=NX - o),
            )
            xcopy[k].start()

    ring_copies = []

    def ring_copy(k, way, hop):
        lo, hi = COL[k], COL[k] + CHUNKS[k][2]
        if way == 0:
            src, dst, to = (NZ + 1 - hop) % NZ, NZ - hop, dev(dz=1)
        else:
            src, dst, to = hop - 1, hop, dev(dz=NZ - 1)
        n = (k * 2 + way) * 4 + hop - 1
        return remote(
            rows.at[src * TOK : (src + 1) * TOK, lo:hi], rows.at[dst * TOK : (dst + 1) * TOK, lo:hi],
            rs.at[n], rr.at[n], to,
        )

    def ring(k, hop):
        if hop == 0:
            if k in own:
                own[k].wait()
            else:
                xcopy[k].wait_recv()
        for way in range(2):
            if 0 < hop <= HOPS[k][way]:
                ring_copy(k, way, hop).wait_recv()
            if hop < HOPS[k][way]:
                copy = ring_copy(k, way, hop + 1)
                copy.start()
                ring_copies.append(copy)

    gcopy = []

    def send_gates():
        for o in range(1, NX):
            mcopy[o].wait_recv()
        for d in range(1, NZ):
            copy = remote(meta.at[:, d], plane.at[:, NZ - d], gs.at[d], gr.at[d], dev(dz=d))
            copy.start()
            gcopy.append(copy)
        plane[:, 0] = meta[:, 0]

    def make_targets():
        for copy in gcopy:
            copy.wait_recv()
        a = lax.broadcasted_iota(I32, (TOK, TOK), 0)
        b = lax.broadcasted_iota(I32, (TOK, TOK), 1)
        earlier = jnp.where(a < b, 1.0, 0.0).astype(BF16)
        n = NZ * GROUPS
        base = CAP * (lax.broadcasted_iota(I32, (n, TOK), 0) // GROUPS)
        for o in range(NX):
            chosen = plane[o].reshape(n, TOK) != 0.0
            position = jnp.dot(jnp.where(chosen, 1.0, 0.0).astype(BF16), earlier, preferred_element_type=F32)
            target[o] = jnp.where(chosen, position.astype(I32) + base, -1).reshape(NZ, GROUPS, TOK)

    ycopies = {}

    def ycopy(k, j):
        lo, w = COL[k], CHUNKS[k][2]
        dc, dy = j // NY, lax.rem(j, NY)
        group = dc * NY + lax.rem(NY - dy, NY)
        n = k * GROUPS + j
        return remote(
            sendbuf.at[k % NSB, j, :, 0:w],
            routed.at[pl.ds(pl.multiple_of(group * PART, 16), PART), lo : lo + w],
            ys.at[n], yr.at[n], dev(dc=dc, dy=dy),
        )

    def select(k):
        o, _, w = CHUNKS[k]
        lo = COL[k]
        if k >= NSB:
            for j in range(1, GROUPS):
                ycopy(k - NSB, j).wait_send()
        slot = lax.broadcasted_iota(I32, (PART, TOK), 0)

        def picked(j):
            hits, gate = [], jnp.zeros((PART, TOK), F32)
            for d in range(NZ):
                hit = slot == target[o, d, pl.ds(j, 1), :]
                hits.append(jnp.where(hit, 1.0, 0.0).astype(BF16))
                gate += jnp.where(hit, plane[o, d, pl.ds(j, 1), :], 0.0)
            gate = jnp.sum(gate, axis=1, keepdims=True)
            chosen = jnp.dot(
                jnp.concatenate(hits, axis=1), rows[:, lo : lo + w], preferred_element_type=F32
            )
            return (chosen * gate).astype(BF16)

        def one(j, _):
            sendbuf[k % NSB, j, :, 0:w] = picked(j)
            ycopy(k, j).start()
            return 0

        lax.fori_loop(1, GROUPS, one, 0)
        routed[0:PART, lo : lo + w] = picked(0)

    def arrived(k):
        for j in range(1, GROUPS):
            ycopy(k, j).wait_recv()

    def hidden_product(k, fresh):
        _, first, w = CHUNKS[k]
        lo = COL[k]

        def one(t, _):
            at = pl.ds(pl.multiple_of(t * TILE, TILE), TILE)
            got = jnp.dot(routed[at, lo : lo + w], wts[first : first + w, :], preferred_element_type=F32)
            acc[at, :] = got if fresh else acc[at, :] + got
            return 0

        lax.fori_loop(0, SLOTS // TILE, one, 0)

    def weight_product(k, fresh):
        o, first, w = CHUNKS[k]
        lo = COL[k]

        def one(t, _):
            got = lax.dot_general(
                routed[:, pl.ds(pl.multiple_of(lo + t * TILE, TILE), TILE)], hid[o],
                (((0,), (0,)), ((), ())), preferred_element_type=F32,
            )
            at = pl.ds(pl.multiple_of(first + t * TILE, TILE), TILE)
            wg_out[0, at, :] = got if fresh else wg_out[0, at, :] + got
            return 0

        lax.fori_loop(0, w // TILE, one, 0)

    def origin(n):
        block = ((n.astype(F32) + 0.5) * (1.0 / CAP)).astype(I32)
        slot = n - block * CAP
        group = ((block.astype(F32) + 0.5) * (1.0 / NZ)).astype(I32)
        d = block - group * NZ
        dc = jnp.where(group >= NY, 1, 0)
        dy = group - dc * NY
        dz = z + d
        dz = jnp.where(dz >= NZ, dz - NZ, dz)
        dy = y + dy
        dy = jnp.where(dy >= NY, dy - NY, dy)
        dc = c + dc
        dc = jnp.where(dc >= NC, dc - NC, dc)
        return CAP * (dz * GROUPS + dc * NY + dy) + slot

    hcopy = {}

    def send_hidden():
        load_hidden.wait()

        def one(t, _):
            n = lax.broadcasted_iota(I32, (TILE, 1), 0) + t * TILE
            m = lax.broadcasted_iota(I32, (TILE, SLOTS), 1)
            pick = jnp.where(origin(n) == m, 1.0, 0.0).astype(BF16)
            at = pl.ds(pl.multiple_of(t * TILE, TILE), TILE)
            hid[0, at, :] = jnp.dot(pick, raw[...], preferred_element_type=F32).astype(BF16)
            return 0

        lax.fori_loop(0, SLOTS // TILE, one, 0)
        hcopy[0] = remote(hid.at[0], hid.at[3], hs.at[0], hr.at[0], dev(dx=1))
        hcopy[1] = remote(hid.at[0], hid.at[1], hs.at[1], hr.at[1], dev(dx=NX - 1))
        hcopy[0].start()
        hcopy[1].start()

    def pass_hidden():
        hcopy[0].wait_recv()
        hcopy[2] = remote(hid.at[3, 0:HALF], hid.at[2, 0:HALF], hs.at[2], hr.at[2], dev(dx=1))
        hcopy[2].start()
        hcopy[1].wait_recv()
        hcopy[3] = remote(hid.at[1, HALF:SLOTS], hid.at[2, HALF:SLOTS], hs.at[3], hr.at[3], dev(dx=NX - 1))
        hcopy[3].start()

    def got_far_hidden():
        hcopy[2].wait_recv()
        hcopy[3].wait_recv()

    pcopy = {}

    def send_far():
        part[1] = acc[...].astype(BF16)
        pcopy[0] = remote(part.at[1, 0:HALF], part2.at[0], ps.at[0], pr.at[0], dev(dx=1))
        pcopy[1] = remote(part.at[1, HALF:SLOTS], part2.at[1], ps.at[1], pr.at[1], dev(dx=NX - 1))
        pcopy[0].start()
        pcopy[1].start()

    def send_near(way):
        pcopy[way].wait_recv()
        if way == 0:
            part[0, 0:HALF] = (acc[0:HALF] + part2[0].astype(F32)).astype(BF16)
            part[0, HALF:SLOTS] = acc[HALF:SLOTS].astype(BF16)
            pcopy[2] = remote(part.at[0], partr.at[0], ps.at[2], pr.at[2], dev(dx=1))
            pcopy[2].start()
        else:
            part[2, 0:HALF] = acc[0:HALF].astype(BF16)
            part[2, HALF:SLOTS] = (acc[HALF:SLOTS] + part2[1].astype(F32)).astype(BF16)
            pcopy[3] = remote(part.at[2], partr.at[1], ps.at[3], pr.at[3], dev(dx=NX - 1))
            pcopy[3].start()

    def finish():
        pcopy[2].wait_recv()
        pcopy[3].wait_recv()
        total = acc[...] + partr[0].astype(F32) + partr[1].astype(F32)
        part[1] = total.astype(BF16)

        def one(t, _):
            n = lax.broadcasted_iota(I32, (1, SLOTS), 1)
            m = lax.broadcasted_iota(I32, (TILE, SLOTS), 0) + t * TILE
            pick = jnp.where(origin(n) == m, 1.0, 0.0).astype(BF16)
            at = pl.ds(pl.multiple_of(t * TILE, TILE), TILE)
            dh_out[0, 0, at, :] = jnp.dot(pick, part[1], preferred_element_type=F32).astype(BF16)
            return 0

        lax.fori_loop(0, SLOTS // TILE, one, 0)

    started = {}

    def weight_step(k):
        o, first, w = CHUNKS[k]
        fresh = first not in started
        started[first] = True
        weight_product(k, fresh)

    def main(k):
        arrived(k)
        if k == 0:
            wg_out[...] = jnp.zeros_like(wg_out)
            weight_product(0, False)
        elif k in (1, 2):
            if k == 1:
                load_weight.wait()
            hidden_product(k, k == 1)
            if k == 2:
                send_far()
        elif k in (3, 4):
            hidden_product(k, k == 3)
            if k == 4:
                send_near(0)
            weight_product(k, False)
        elif k in (5, 6):
            hidden_product(k, k == 5)
            if k == 6:
                send_near(1)
                pcopy[0].wait_send()
                pcopy[1].wait_send()
                weight_product(5, False)
                weight_product(6, False)
            else:
                got_far_hidden()
                weight_product(1, False)
                weight_product(2, False)
        else:
            if k == 7:
                hidden_product(0, True)
            hidden_product(k, False)
            weight_product(k, False)

    for q in range(2 * NK + 7):
        for k in range(NK):
            if 0 <= q - 2 * k <= 4:
                ring(k, q - 2 * k)
        if q == 0:
            send_gates()
        if q == 1:
            send_hidden()
        if q == 2:
            make_targets()
        k, odd = divmod(q - 4, 2)
        if 0 <= k < NK and not odd:
            select(k)
        k, odd = divmod(q - 7, 2)
        if 0 <= k < NK and not odd:
            main(k)
        if q == 8:
            pass_hidden()
    finish()

    for o in range(1, NX):
        mcopy[o].wait_send()
    for k in xcopy:
        xcopy[k].wait_send()
    for copy in gcopy + ring_copies:
        copy.wait_send()
    for k in range(max(0, NK - NSB), NK):
        for j in range(1, GROUPS):
            ycopy(k, j).wait_send()
    for n in range(4):
        hcopy[n].wait_send()
    pcopy[2].wait_send()
    pcopy[3].wait_send()


def body(d_out, route_ids, gate_weights, saved_hidden, down_weight):
    ids_t = route_ids[0].T
    gate_t = gate_weights[0].T
    vmem = pl.BlockSpec(memory_space=pltpu.VMEM)
    hbm = pl.BlockSpec(memory_space=pl.ANY)
    dma = pltpu.SemaphoreType.DMA
    return pl.pallas_call(
        kernel,
        out_shape=(
            jax.ShapeDtypeStruct((1, 1, SLOTS, FF), BF16),
            jax.ShapeDtypeStruct((1, WIDTH, FF), F32),
        ),
        in_specs=[hbm, vmem, vmem, hbm, hbm],
        out_specs=(vmem, vmem),
        scratch_shapes=[
            pltpu.VMEM((NZ * TOK, NX * WIDTH), BF16),
            pltpu.VMEM((NSB, GROUPS, PART, WMAX), BF16),
            pltpu.VMEM((SLOTS, NX * WIDTH), BF16),
            pltpu.VMEM((NX, SLOTS, FF), BF16),
            pltpu.VMEM((SLOTS, FF), BF16),
            pltpu.VMEM((WIDTH, FF), BF16),
            pltpu.VMEM((SLOTS, FF), F32),
            pltpu.VMEM((3, SLOTS, FF), BF16),
            pltpu.VMEM((2, HALF, FF), BF16),
            pltpu.VMEM((2, SLOTS, FF), BF16),
            pltpu.VMEM((NX, NZ, GROUPS, TOK), F32),
            pltpu.VMEM((NX, NZ, GROUPS, TOK), F32),
            pltpu.VMEM((NX, NZ, GROUPS, TOK), I32),
            dma((2 + NK,)),
            dma((NK,)), dma((NK,)),
            dma((NX,)), dma((NX,)),
            dma((NZ,)), dma((NZ,)),
            dma((NK * 8,)), dma((NK * 8,)),
            dma((NK * GROUPS,)), dma((NK * GROUPS,)),
            dma((4,)), dma((4,)),
            dma((4,)), dma((4,)),
        ],
        compiler_params=pltpu.CompilerParams(
            collective_id=0, has_side_effects=True, vmem_limit_bytes=62 * 2**20
        ),
        name="expert_backward",
    )(d_out, ids_t, gate_t, saved_hidden, down_weight)


def solution(mesh):
    return jax.shard_map(
        body,
        mesh=mesh,
        in_specs=(
            P("dp", ("ctx", "exp"), None),
            P("dp", ("ctx", "exp"), None),
            P("dp", ("ctx", "exp"), None),
            P("dp", ("ctx", "exp"), None, None),
            P(("ctx", "exp"), "dp", None),
        ),
        out_specs=(P("dp", ("ctx", "exp"), None, None), P(("ctx", "exp"), "dp", None)),
        check_vma=False,
    )
```

```python
import functools

import jax
import jax.numpy as jnp
from jax import lax
from jax.experimental import pallas as pl
from jax.experimental.pallas import tpu as pltpu
from jax.sharding import PartitionSpec as P

MESH = pl.DeviceIdType.MESH
F32, BF16, I32 = jnp.float32, jnp.bfloat16, jnp.int32

NX, NY, NZ, NC = 4, 4, 8, 2
TOK, CAP, FF = 128, 14, 768
GROUPS = NY * NC
PART = NZ * CAP
SLOTS = GROUPS * PART
WIDTH = 1280
HALF = SLOTS // 2
TILE = 128

CHUNKS = (
    (2, 0, 256),
    (2, 256, 384),
    (2, 640, 640),
    (1, 0, 640),
    (1, 640, 640),
    (3, 0, 640),
    (3, 640, 640),
    (0, 0, 640),
    (0, 640, 384),
    (0, 1024, 256),
)
NK = len(CHUNKS)
COL = [sum(c[2] for c in CHUNKS[:k]) for k in range(NK)]
WMAX = max(c[2] for c in CHUNKS)
NSB = 3
LAST = NZ // 2
MAIN_LAG = 7
HIDDEN_AT, PASS_AT = 5, 10
FEATURES_AT = {0: (1, 2), 2: (3,), 4: (4,), 6: (5, 6)}


def kernel(
    d_out, ids_t, gate_t, hidden, weight, dh_out, wg_out,
    rows, sendbuf, routed, hid, raw, wts, acc, part, part2, partr,
    meta, plane, target,
    loc_sem, xs, xr, ms, mr, gs, gr, rs, rr, ys, yr, hs, hr, ps, pr,
):
    i = lax.axis_index("dp")
    ctx = lax.axis_index("ctx")
    y = lax.axis_index("exp")
    z = ctx // NC
    c = lax.rem(ctx, NC)

    def dev(dx=0, dz=0, dc=0, dy=0):
        return (
            lax.rem(i + dx, NX),
            lax.rem(z + dz, NZ) * NC + lax.rem(c + dc, NC),
            lax.rem(y + dy, NY),
        )

    def remote(src, dst, send, recv, to):
        return pltpu.make_async_remote_copy(
            src_ref=src, dst_ref=dst, send_sem=send, recv_sem=recv, device_id=to, device_id_type=MESH
        )

    load_hidden = pltpu.make_async_copy(hidden.at[0, 0], raw, loc_sem.at[0])
    load_hidden.start()
    load_weight = pltpu.make_async_copy(weight.at[0], wts, loc_sem.at[1])
    load_weight.start()
    own = {}
    for k, (o, first, w) in enumerate(CHUNKS):
        if o == 0:
            start = pl.multiple_of(i * WIDTH + first, 128)
            own[k] = pltpu.make_async_copy(
                d_out.at[0, :, pl.ds(start, w)], rows.at[0:TOK, COL[k] : COL[k] + w], loc_sem.at[2 + k]
            )
            own[k].start()

    barrier = pltpu.get_barrier_semaphore()
    peers = [dict(dx=a) for a in range(1, NX)] + [dict(dz=a) for a in range(1, NZ)]
    peers += [dict(dc=j // NY, dy=j % NY) for j in range(1, GROUPS)]
    for p in peers:
        pl.semaphore_signal(barrier, inc=1, device_id=dev(**p), device_id_type=MESH)

    r = lax.broadcasted_iota(I32, (NZ * GROUPS, TOK), 0)
    dz, dc, dy = r // GROUPS, (r // NY) % NC, r % NY
    expert = ((z + dz) % NZ) * GROUPS + ((c + dc) % NC) * NY + (y + dy) % NY
    gates = jnp.zeros((NZ * GROUPS, TOK), F32)
    for k in range(ids_t.shape[0]):
        gates += jnp.where(ids_t[k : k + 1, :] == expert, gate_t[k : k + 1, :], 0.0)
    meta[0] = gates.reshape(NZ, GROUPS, TOK)

    pl.semaphore_wait(barrier, len(peers))

    xcopy = {}

    def send_features(k):
        o, first, w = CHUNKS[k]
        start = pl.multiple_of(lax.rem(i + NX - o, NX) * WIDTH + first, 128)
        xcopy[k] = remote(
            d_out.at[0, :, pl.ds(start, w)], rows.at[0:TOK, COL[k] : COL[k] + w],
            xs.at[k], xr.at[k], dev(dx=NX - o),
        )
        xcopy[k].start()

    send_features(0)
    mcopy = {}
    for o in range(1, NX):
        mcopy[o] = remote(meta.at[0], meta.at[o], ms.at[o], mr.at[o], dev(dx=NX - o))
        mcopy[o].start()

    ring_copies = []

    def ring_copy(k, way, hop):
        lo, hi = COL[k], COL[k] + CHUNKS[k][2]
        if way == 0:
            src, dst, to = (NZ + 1 - hop) % NZ, NZ - hop, dev(dz=1)
        else:
            src, dst, to = hop - 1, hop, dev(dz=NZ - 1)
        first, n = 0, TOK
        if hop == LAST:
            first, n = way * (TOK // 2), TOK // 2
        src, dst = src * TOK + first, dst * TOK + first
        sem = (k * 2 + way) * LAST + hop - 1
        return remote(rows.at[src : src + n, lo:hi], rows.at[dst : dst + n, lo:hi], rs.at[sem], rr.at[sem], to)

    def ring(k, hop):
        if hop == 0:
            if k in own:
                own[k].wait()
            else:
                xcopy[k].wait_recv()
        for way in range(2):
            if hop > 0:
                ring_copy(k, way, hop).wait_recv()
            if hop < LAST:
                copy = ring_copy(k, way, hop + 1)
                copy.start()
                ring_copies.append(copy)

    gcopy = []

    def send_gates():
        for o in range(1, NX):
            mcopy[o].wait_recv()
        for d in range(1, NZ):
            copy = remote(meta.at[:, d], plane.at[:, NZ - d], gs.at[d], gr.at[d], dev(dz=d))
            copy.start()
            gcopy.append(copy)
        plane[:, 0] = meta[:, 0]

    def make_targets():
        for copy in gcopy:
            copy.wait_recv()
        a = lax.broadcasted_iota(I32, (TOK, TOK), 0)
        b = lax.broadcasted_iota(I32, (TOK, TOK), 1)
        earlier = jnp.where(a < b, 1.0, 0.0).astype(BF16)
        n = NZ * GROUPS
        base = CAP * (lax.broadcasted_iota(I32, (n, TOK), 0) // GROUPS)
        for o in range(NX):
            chosen = plane[o].reshape(n, TOK) != 0.0
            position = jnp.dot(jnp.where(chosen, 1.0, 0.0).astype(BF16), earlier, preferred_element_type=F32)
            target[o] = jnp.where(chosen, position.astype(I32) + base, -1).reshape(NZ, GROUPS, TOK)

    ycopies = {}

    def ycopy(k, j):
        lo, w = COL[k], CHUNKS[k][2]
        dc, dy = j // NY, lax.rem(j, NY)
        group = dc * NY + lax.rem(NY - dy, NY)
        n = k * GROUPS + j
        return remote(
            sendbuf.at[k % NSB, j, :, 0:w],
            routed.at[pl.ds(pl.multiple_of(group * PART, 16), PART), lo : lo + w],
            ys.at[n], yr.at[n], dev(dc=dc, dy=dy),
        )

    def select(k):
        o, _, w = CHUNKS[k]
        lo = COL[k]
        if k >= NSB:
            for j in range(1, GROUPS):
                ycopy(k - NSB, j).wait_send()
        slot = lax.broadcasted_iota(I32, (PART, TOK), 0)

        def picked(j):
            hits, gate = [], jnp.zeros((PART, TOK), F32)
            for d in range(NZ):
                hit = slot == target[o, d, pl.ds(j, 1), :]
                hits.append(jnp.where(hit, 1.0, 0.0).astype(BF16))
                gate += jnp.where(hit, plane[o, d, pl.ds(j, 1), :], 0.0)
            gate = jnp.sum(gate, axis=1, keepdims=True)
            chosen = jnp.dot(
                jnp.concatenate(hits, axis=1), rows[:, lo : lo + w], preferred_element_type=F32
            )
            return (chosen * gate).astype(BF16)

        def one(j, _):
            sendbuf[k % NSB, j, :, 0:w] = picked(j)
            ycopy(k, j).start()
            return 0

        lax.fori_loop(1, GROUPS, one, 0)
        routed[0:PART, lo : lo + w] = picked(0)

    def arrived(k):
        for j in range(1, GROUPS):
            ycopy(k, j).wait_recv()

    def hidden_product(k, fresh):
        _, first, w = CHUNKS[k]
        lo = COL[k]

        def one(t, _):
            at = pl.ds(pl.multiple_of(t * TILE, TILE), TILE)
            got = jnp.dot(routed[at, lo : lo + w], wts[first : first + w, :], preferred_element_type=F32)
            acc[at, :] = got if fresh else acc[at, :] + got
            return 0

        lax.fori_loop(0, SLOTS // TILE, one, 0)

    def weight_product(k):
        o, first, w = CHUNKS[k]
        lo = COL[k]

        def one(t, _):
            got = lax.dot_general(
                routed[:, pl.ds(pl.multiple_of(lo + t * TILE, TILE), TILE)], hid[o],
                (((0,), (0,)), ((), ())), preferred_element_type=F32,
            )
            at = pl.ds(pl.multiple_of(first + t * TILE, TILE), TILE)
            wg_out[0, at, :] += got
            return 0

        lax.fori_loop(0, w // TILE, one, 0)

    def origin(n):
        block = ((n.astype(F32) + 0.5) * (1.0 / CAP)).astype(I32)
        slot = n - block * CAP
        group = ((block.astype(F32) + 0.5) * (1.0 / NZ)).astype(I32)
        d = block - group * NZ
        dc = jnp.where(group >= NY, 1, 0)
        dy = group - dc * NY
        dz = z + d
        dz = jnp.where(dz >= NZ, dz - NZ, dz)
        dy = y + dy
        dy = jnp.where(dy >= NY, dy - NY, dy)
        dc = c + dc
        dc = jnp.where(dc >= NC, dc - NC, dc)
        return CAP * (dz * GROUPS + dc * NY + dy) + slot

    hcopy = {}

    def send_hidden():
        load_hidden.wait()

        def one(t, _):
            n = lax.broadcasted_iota(I32, (TILE, 1), 0) + t * TILE
            m = lax.broadcasted_iota(I32, (TILE, SLOTS), 1)
            pick = jnp.where(origin(n) == m, 1.0, 0.0).astype(BF16)
            at = pl.ds(pl.multiple_of(t * TILE, TILE), TILE)
            hid[0, at, :] = jnp.dot(pick, raw[...], preferred_element_type=F32).astype(BF16)
            return 0

        lax.fori_loop(0, SLOTS // TILE, one, 0)
        hcopy[0] = remote(hid.at[0], hid.at[3], hs.at[0], hr.at[0], dev(dx=1))
        hcopy[1] = remote(hid.at[0], hid.at[1], hs.at[1], hr.at[1], dev(dx=NX - 1))
        hcopy[0].start()
        hcopy[1].start()

    def pass_hidden():
        hcopy[0].wait_recv()
        hcopy[2] = remote(hid.at[3, 0:HALF], hid.at[2, 0:HALF], hs.at[2], hr.at[2], dev(dx=1))
        hcopy[2].start()
        hcopy[1].wait_recv()
        hcopy[3] = remote(hid.at[1, HALF:SLOTS], hid.at[2, HALF:SLOTS], hs.at[3], hr.at[3], dev(dx=NX - 1))
        hcopy[3].start()

    def got_far_hidden():
        hcopy[2].wait_recv()
        hcopy[3].wait_recv()

    pcopy = {}

    def send_far():
        part[1] = acc[...].astype(BF16)
        pcopy[0] = remote(part.at[1, 0:HALF], part2.at[0], ps.at[0], pr.at[0], dev(dx=1))
        pcopy[1] = remote(part.at[1, HALF:SLOTS], part2.at[1], ps.at[1], pr.at[1], dev(dx=NX - 1))
        pcopy[0].start()
        pcopy[1].start()

    def send_near(way):
        pcopy[way].wait_recv()
        if way == 0:
            part[0, 0:HALF] = (acc[0:HALF] + part2[0].astype(F32)).astype(BF16)
            part[0, HALF:SLOTS] = acc[HALF:SLOTS].astype(BF16)
            pcopy[2] = remote(part.at[0], partr.at[0], ps.at[2], pr.at[2], dev(dx=1))
            pcopy[2].start()
        else:
            part[2, 0:HALF] = acc[0:HALF].astype(BF16)
            part[2, HALF:SLOTS] = (acc[HALF:SLOTS] + part2[1].astype(F32)).astype(BF16)
            pcopy[3] = remote(part.at[2], partr.at[1], ps.at[3], pr.at[3], dev(dx=NX - 1))
            pcopy[3].start()

    def finish():
        pcopy[2].wait_recv()
        pcopy[3].wait_recv()
        total = acc[...] + partr[0].astype(F32) + partr[1].astype(F32)
        part[1] = total.astype(BF16)

        def one(t, _):
            n = lax.broadcasted_iota(I32, (1, SLOTS), 1)
            m = lax.broadcasted_iota(I32, (TILE, SLOTS), 0) + t * TILE
            pick = jnp.where(origin(n) == m, 1.0, 0.0).astype(BF16)
            at = pl.ds(pl.multiple_of(t * TILE, TILE), TILE)
            dh_out[0, 0, at, :] = jnp.dot(pick, part[1], preferred_element_type=F32).astype(BF16)
            return 0

        lax.fori_loop(0, SLOTS // TILE, one, 0)

    for first in range(0, WIDTH, TILE):
        wg_out[0, first : first + TILE, :] = jnp.zeros((TILE, FF), F32)

    def main(k):
        o, first, w = CHUNKS[k]
        arrived(k)
        if k == 0:
            load_weight.wait()
        hidden_product(k, first == 0)
        if first + w == WIDTH:
            if o == 2:
                send_far()
            elif o == 1:
                send_near(0)
            elif o == 3:
                send_near(1)
                pcopy[0].wait_send()
                pcopy[1].wait_send()
        if o != 2:
            weight_product(k)
        if (o, first) == (3, 0):
            got_far_hidden()
        if o == 3:
            for m in range(NK):
                if CHUNKS[m][0] == 2 and (CHUNKS[m][1] < WIDTH // 2) == (first == 0):
                    weight_product(m)

    for q in range(2 * NK + MAIN_LAG):
        for k in reversed(range(NK)):
            if 0 <= q - 2 * k <= LAST:
                ring(k, q - 2 * k)
        for k in FEATURES_AT.get(q, ()):
            send_features(k)
        if q == 0:
            send_gates()
        if q == 2:
            make_targets()
        if q == HIDDEN_AT:
            send_hidden()
        if q == PASS_AT:
            pass_hidden()
        k, odd = divmod(q - LAST, 2)
        if 0 <= k < NK and not odd:
            select(k)
        k, odd = divmod(q - MAIN_LAG, 2)
        if 0 <= k < NK and not odd:
            main(k)
    finish()

    for o in range(1, NX):
        mcopy[o].wait_send()
    for k in xcopy:
        xcopy[k].wait_send()
    for copy in gcopy + ring_copies:
        copy.wait_send()
    for k in range(max(0, NK - NSB), NK):
        for j in range(1, GROUPS):
            ycopy(k, j).wait_send()
    for n in range(4):
        hcopy[n].wait_send()
    pcopy[2].wait_send()
    pcopy[3].wait_send()


def body(d_out, route_ids, gate_weights, saved_hidden, down_weight):
    ids_t = route_ids[0].T
    gate_t = gate_weights[0].T
    vmem = pl.BlockSpec(memory_space=pltpu.VMEM)
    hbm = pl.BlockSpec(memory_space=pl.ANY)
    dma = pltpu.SemaphoreType.DMA
    return pl.pallas_call(
        kernel,
        out_shape=(
            jax.ShapeDtypeStruct((1, 1, SLOTS, FF), BF16),
            jax.ShapeDtypeStruct((1, WIDTH, FF), F32),
        ),
        in_specs=[hbm, vmem, vmem, hbm, hbm],
        out_specs=(vmem, vmem),
        scratch_shapes=[
            pltpu.VMEM((NZ * TOK, NX * WIDTH), BF16),
            pltpu.VMEM((NSB, GROUPS, PART, WMAX), BF16),
            pltpu.VMEM((SLOTS, NX * WIDTH), BF16),
            pltpu.VMEM((NX, SLOTS, FF), BF16),
            pltpu.VMEM((SLOTS, FF), BF16),
            pltpu.VMEM((WIDTH, FF), BF16),
            pltpu.VMEM((SLOTS, FF), F32),
            pltpu.VMEM((3, SLOTS, FF), BF16),
            pltpu.VMEM((2, HALF, FF), BF16),
            pltpu.VMEM((2, SLOTS, FF), BF16),
            pltpu.VMEM((NX, NZ, GROUPS, TOK), F32),
            pltpu.VMEM((NX, NZ, GROUPS, TOK), F32),
            pltpu.VMEM((NX, NZ, GROUPS, TOK), I32),
            dma((2 + NK,)),
            dma((NK,)), dma((NK,)),
            dma((NX,)), dma((NX,)),
            dma((NZ,)), dma((NZ,)),
            dma((NK * 8,)), dma((NK * 8,)),
            dma((NK * GROUPS,)), dma((NK * GROUPS,)),
            dma((4,)), dma((4,)),
            dma((4,)), dma((4,)),
        ],
        compiler_params=pltpu.CompilerParams(
            collective_id=0, has_side_effects=True, vmem_limit_bytes=62 * 2**20
        ),
        name="expert_backward",
    )(d_out, ids_t, gate_t, saved_hidden, down_weight)


def solution(mesh):
    return jax.shard_map(
        body,
        mesh=mesh,
        in_specs=(
            P("dp", ("ctx", "exp"), None),
            P("dp", ("ctx", "exp"), None),
            P("dp", ("ctx", "exp"), None),
            P("dp", ("ctx", "exp"), None, None),
            P(("ctx", "exp"), "dp", None),
        ),
        out_specs=(P("dp", ("ctx", "exp"), None, None), P(("ctx", "exp"), "dp", None)),
        check_vma=False,
    )
```

```python
import functools

import jax
import jax.numpy as jnp
from jax import lax
from jax.experimental import pallas as pl
from jax.experimental.pallas import tpu as pltpu
from jax.sharding import PartitionSpec as P

MESH = pl.DeviceIdType.MESH
F32, BF16, I32 = jnp.float32, jnp.bfloat16, jnp.int32

NX, NY, NZ, NC = 4, 4, 8, 2
TOK, CAP, FF = 128, 14, 768
GROUPS = NY * NC
PART = NZ * CAP
SLOTS = GROUPS * PART
WIDTH = 1280
HALF = SLOTS // 2
TILE = 128

CHUNKS = (
    (2, 0, 256),
    (2, 256, 384),
    (2, 640, 640),
    (1, 0, 640),
    (1, 640, 640),
    (3, 0, 640),
    (3, 640, 640),
    (0, 0, 640),
    (0, 640, 384),
    (0, 1024, 256),
)
NK = len(CHUNKS)
COL = [sum(c[2] for c in CHUNKS[:k]) for k in range(NK)]
WMAX = max(c[2] for c in CHUNKS)
NSB = 3
LAST = NZ // 2
MAIN_LAG = 7
HIDDEN_AT, PASS_AT = 4, 9
FEATURES_AT = {0: (1, 2), 2: (3, 4), 3: (5, 6)}


def kernel(
    d_out, ids_t, gate_t, hidden, weight, dh_out, wg_out,
    rows, sendbuf, routed, hid, raw, wts, acc, part, part2, partr,
    meta, plane, target,
    loc_sem, xs, xr, ms, mr, gs, gr, rs, rr, ys, yr, hs, hr, ps, pr,
):
    i = lax.axis_index("dp")
    ctx = lax.axis_index("ctx")
    y = lax.axis_index("exp")
    z = ctx // NC
    c = lax.rem(ctx, NC)

    def dev(dx=0, dz=0, dc=0, dy=0):
        return (
            lax.rem(i + dx, NX),
            lax.rem(z + dz, NZ) * NC + lax.rem(c + dc, NC),
            lax.rem(y + dy, NY),
        )

    def remote(src, dst, send, recv, to):
        return pltpu.make_async_remote_copy(
            src_ref=src, dst_ref=dst, send_sem=send, recv_sem=recv, device_id=to, device_id_type=MESH
        )

    load_hidden = pltpu.make_async_copy(hidden.at[0, 0], raw, loc_sem.at[0])
    load_hidden.start()
    load_weight = pltpu.make_async_copy(weight.at[0], wts, loc_sem.at[1])
    load_weight.start()
    own = {}
    for k, (o, first, w) in enumerate(CHUNKS):
        if o == 0:
            start = pl.multiple_of(i * WIDTH + first, 128)
            own[k] = pltpu.make_async_copy(
                d_out.at[0, :, pl.ds(start, w)], rows.at[0:TOK, COL[k] : COL[k] + w], loc_sem.at[2 + k]
            )
            own[k].start()

    barrier = pltpu.get_barrier_semaphore()
    peers = [dict(dx=a) for a in range(1, NX)] + [dict(dz=a) for a in range(1, NZ)]
    peers += [dict(dc=j // NY, dy=j % NY) for j in range(1, GROUPS)]
    for p in peers:
        pl.semaphore_signal(barrier, inc=1, device_id=dev(**p), device_id_type=MESH)

    r = lax.broadcasted_iota(I32, (NZ * GROUPS, TOK), 0)
    dz, dc, dy = r // GROUPS, (r // NY) % NC, r % NY
    expert = ((z + dz) % NZ) * GROUPS + ((c + dc) % NC) * NY + (y + dy) % NY
    gates = jnp.zeros((NZ * GROUPS, TOK), F32)
    for k in range(ids_t.shape[0]):
        gates += jnp.where(ids_t[k : k + 1, :] == expert, gate_t[k : k + 1, :], 0.0)
    meta[0] = gates.reshape(NZ, GROUPS, TOK)

    pl.semaphore_wait(barrier, len(peers))

    xcopy = {}

    def send_features(k):
        o, first, w = CHUNKS[k]
        start = pl.multiple_of(lax.rem(i + NX - o, NX) * WIDTH + first, 128)
        xcopy[k] = remote(
            d_out.at[0, :, pl.ds(start, w)], rows.at[0:TOK, COL[k] : COL[k] + w],
            xs.at[k], xr.at[k], dev(dx=NX - o),
        )
        xcopy[k].start()

    send_features(0)
    mcopy = {}
    for o in range(1, NX):
        mcopy[o] = remote(meta.at[0], meta.at[o], ms.at[o], mr.at[o], dev(dx=NX - o))
        mcopy[o].start()

    ring_copies = []

    def ring_copy(k, way, hop):
        lo, hi = COL[k], COL[k] + CHUNKS[k][2]
        if way == 0:
            src, dst, to = (NZ + 1 - hop) % NZ, NZ - hop, dev(dz=1)
        else:
            src, dst, to = hop - 1, hop, dev(dz=NZ - 1)
        first, n = 0, TOK
        if hop == LAST:
            first, n = way * (TOK // 2), TOK // 2
        src, dst = src * TOK + first, dst * TOK + first
        sem = (k * 2 + way) * LAST + hop - 1
        return remote(rows.at[src : src + n, lo:hi], rows.at[dst : dst + n, lo:hi], rs.at[sem], rr.at[sem], to)

    def ring(k, hop):
        if hop == 0:
            if k in own:
                own[k].wait()
            else:
                xcopy[k].wait_recv()
        for way in range(2):
            if hop > 0:
                ring_copy(k, way, hop).wait_recv()
            if hop < LAST:
                copy = ring_copy(k, way, hop + 1)
                copy.start()
                ring_copies.append(copy)

    gcopy = []

    def send_gates():
        for o in range(1, NX):
            mcopy[o].wait_recv()
        for d in range(1, NZ):
            copy = remote(meta.at[:, d], plane.at[:, NZ - d], gs.at[d], gr.at[d], dev(dz=d))
            copy.start()
            gcopy.append(copy)
        plane[:, 0] = meta[:, 0]

    def make_targets():
        for copy in gcopy:
            copy.wait_recv()
        a = lax.broadcasted_iota(I32, (TOK, TOK), 0)
        b = lax.broadcasted_iota(I32, (TOK, TOK), 1)
        earlier = jnp.where(a < b, 1.0, 0.0).astype(BF16)
        n = NZ * GROUPS
        base = CAP * (lax.broadcasted_iota(I32, (n, TOK), 0) // GROUPS)
        for o in range(NX):
            chosen = plane[o].reshape(n, TOK) != 0.0
            position = jnp.dot(jnp.where(chosen, 1.0, 0.0).astype(BF16), earlier, preferred_element_type=F32)
            target[o] = jnp.where(chosen, position.astype(I32) + base, -1).reshape(NZ, GROUPS, TOK)

    ycopies = {}

    def ycopy(k, j):
        lo, w = COL[k], CHUNKS[k][2]
        dc, dy = j // NY, lax.rem(j, NY)
        group = dc * NY + lax.rem(NY - dy, NY)
        n = k * GROUPS + j
        return remote(
            sendbuf.at[k % NSB, j, :, 0:w],
            routed.at[pl.ds(pl.multiple_of(group * PART, 16), PART), lo : lo + w],
            ys.at[n], yr.at[n], dev(dc=dc, dy=dy),
        )

    def select(k):
        o, _, w = CHUNKS[k]
        lo = COL[k]
        if k >= NSB:
            for j in range(1, GROUPS):
                ycopy(k - NSB, j).wait_send()
        slot = lax.broadcasted_iota(I32, (PART, TOK), 0)

        def picked(j):
            hits, gate = [], jnp.zeros((PART, TOK), F32)
            for d in range(NZ):
                hit = slot == target[o, d, pl.ds(j, 1), :]
                hits.append(jnp.where(hit, 1.0, 0.0).astype(BF16))
                gate += jnp.where(hit, plane[o, d, pl.ds(j, 1), :], 0.0)
            gate = jnp.sum(gate, axis=1, keepdims=True)
            chosen = jnp.dot(
                jnp.concatenate(hits, axis=1), rows[:, lo : lo + w], preferred_element_type=F32
            )
            return (chosen * gate).astype(BF16)

        def one(j, _):
            sendbuf[k % NSB, j, :, 0:w] = picked(j)
            ycopy(k, j).start()
            return 0

        lax.fori_loop(1, GROUPS, one, 0)
        routed[0:PART, lo : lo + w] = picked(0)

    def arrived(k):
        for j in range(1, GROUPS):
            ycopy(k, j).wait_recv()

    def hidden_product(k, fresh):
        _, first, w = CHUNKS[k]
        lo = COL[k]

        def one(t, _):
            at = pl.ds(pl.multiple_of(t * TILE, TILE), TILE)
            got = jnp.dot(routed[at, lo : lo + w], wts[first : first + w, :], preferred_element_type=F32)
            acc[at, :] = got if fresh else acc[at, :] + got
            return 0

        lax.fori_loop(0, SLOTS // TILE, one, 0)

    def weight_product(k):
        o, first, w = CHUNKS[k]
        lo = COL[k]

        def one(t, _):
            got = lax.dot_general(
                routed[:, pl.ds(pl.multiple_of(lo + t * TILE, TILE), TILE)], hid[o],
                (((0,), (0,)), ((), ())), preferred_element_type=F32,
            )
            at = pl.ds(pl.multiple_of(first + t * TILE, TILE), TILE)
            wg_out[0, at, :] += got
            return 0

        lax.fori_loop(0, w // TILE, one, 0)

    def origin(n):
        block = ((n.astype(F32) + 0.5) * (1.0 / CAP)).astype(I32)
        slot = n - block * CAP
        group = ((block.astype(F32) + 0.5) * (1.0 / NZ)).astype(I32)
        d = block - group * NZ
        dc = jnp.where(group >= NY, 1, 0)
        dy = group - dc * NY
        dz = z + d
        dz = jnp.where(dz >= NZ, dz - NZ, dz)
        dy = y + dy
        dy = jnp.where(dy >= NY, dy - NY, dy)
        dc = c + dc
        dc = jnp.where(dc >= NC, dc - NC, dc)
        return CAP * (dz * GROUPS + dc * NY + dy) + slot

    hcopy = {}

    def send_hidden():
        load_hidden.wait()

        def one(t, _):
            n = lax.broadcasted_iota(I32, (TILE, 1), 0) + t * TILE
            m = lax.broadcasted_iota(I32, (TILE, SLOTS), 1)
            pick = jnp.where(origin(n) == m, 1.0, 0.0).astype(BF16)
            at = pl.ds(pl.multiple_of(t * TILE, TILE), TILE)
            hid[0, at, :] = jnp.dot(pick, raw[...], preferred_element_type=F32).astype(BF16)
            return 0

        lax.fori_loop(0, SLOTS // TILE, one, 0)
        hcopy[0] = remote(hid.at[0], hid.at[3], hs.at[0], hr.at[0], dev(dx=1))
        hcopy[1] = remote(hid.at[0], hid.at[1], hs.at[1], hr.at[1], dev(dx=NX - 1))
        hcopy[0].start()
        hcopy[1].start()

    def pass_hidden():
        hcopy[0].wait_recv()
        hcopy[2] = remote(hid.at[3, 0:HALF], hid.at[2, 0:HALF], hs.at[2], hr.at[2], dev(dx=1))
        hcopy[2].start()
        hcopy[1].wait_recv()
        hcopy[3] = remote(hid.at[1, HALF:SLOTS], hid.at[2, HALF:SLOTS], hs.at[3], hr.at[3], dev(dx=NX - 1))
        hcopy[3].start()

    def got_far_hidden():
        hcopy[2].wait_recv()
        hcopy[3].wait_recv()

    pcopy = {}

    def send_far():
        part[1] = acc[...].astype(BF16)
        pcopy[0] = remote(part.at[1, 0:HALF], part2.at[0], ps.at[0], pr.at[0], dev(dx=1))
        pcopy[1] = remote(part.at[1, HALF:SLOTS], part2.at[1], ps.at[1], pr.at[1], dev(dx=NX - 1))
        pcopy[0].start()
        pcopy[1].start()

    def send_near(way):
        pcopy[way].wait_recv()
        if way == 0:
            part[0, 0:HALF] = (acc[0:HALF] + part2[0].astype(F32)).astype(BF16)
            part[0, HALF:SLOTS] = acc[HALF:SLOTS].astype(BF16)
            pcopy[2] = remote(part.at[0], partr.at[0], ps.at[2], pr.at[2], dev(dx=1))
            pcopy[2].start()
        else:
            part[2, 0:HALF] = acc[0:HALF].astype(BF16)
            part[2, HALF:SLOTS] = (acc[HALF:SLOTS] + part2[1].astype(F32)).astype(BF16)
            pcopy[3] = remote(part.at[2], partr.at[1], ps.at[3], pr.at[3], dev(dx=NX - 1))
            pcopy[3].start()

    def finish():
        pcopy[2].wait_recv()
        pcopy[3].wait_recv()
        total = acc[...] + partr[0].astype(F32) + partr[1].astype(F32)
        part[1] = total.astype(BF16)

        def one(t, _):
            n = lax.broadcasted_iota(I32, (1, SLOTS), 1)
            m = lax.broadcasted_iota(I32, (TILE, SLOTS), 0) + t * TILE
            pick = jnp.where(origin(n) == m, 1.0, 0.0).astype(BF16)
            at = pl.ds(pl.multiple_of(t * TILE, TILE), TILE)
            dh_out[0, 0, at, :] = jnp.dot(pick, part[1], preferred_element_type=F32).astype(BF16)
            return 0

        lax.fori_loop(0, SLOTS // TILE, one, 0)

    def main(k):
        o, first, w = CHUNKS[k]
        arrived(k)
        if k == 0:
            load_weight.wait()
        hidden_product(k, first == 0)
        if first + w == WIDTH:
            if o == 2:
                send_far()
            elif o == 1:
                send_near(0)
            elif o == 3:
                send_near(1)
                pcopy[0].wait_send()
                pcopy[1].wait_send()
        if o != 2:
            weight_product(k)
        if (o, first) == (3, 0):
            got_far_hidden()
        if o == 3:
            for m in range(NK):
                if CHUNKS[m][0] == 2 and (CHUNKS[m][1] < WIDTH // 2) == (first == 0):
                    weight_product(m)

    for q in range(2 * NK + MAIN_LAG):
        for k in reversed(range(NK)):
            if 0 <= q - 2 * k <= LAST:
                ring(k, q - 2 * k)
        for k in FEATURES_AT.get(q, ()):
            send_features(k)
        if q == 0:
            send_gates()
        if q == 1:
            for first in range(0, WIDTH, TILE):
                wg_out[0, first : first + TILE, :] = jnp.zeros((TILE, FF), F32)
        if q == 2:
            make_targets()
        if q == HIDDEN_AT:
            send_hidden()
        if q == PASS_AT:
            pass_hidden()
        k, odd = divmod(q - LAST, 2)
        if 0 <= k < NK and not odd:
            select(k)
        k, odd = divmod(q - MAIN_LAG, 2)
        if 0 <= k < NK and not odd:
            main(k)
    finish()

    for o in range(1, NX):
        mcopy[o].wait_send()
    for k in xcopy:
        xcopy[k].wait_send()
    for copy in gcopy + ring_copies:
        copy.wait_send()
    for k in range(max(0, NK - NSB), NK):
        for j in range(1, GROUPS):
            ycopy(k, j).wait_send()
    for n in range(4):
        hcopy[n].wait_send()
    pcopy[2].wait_send()
    pcopy[3].wait_send()


def body(d_out, route_ids, gate_weights, saved_hidden, down_weight):
    ids_t = route_ids[0].T
    gate_t = gate_weights[0].T
    vmem = pl.BlockSpec(memory_space=pltpu.VMEM)
    hbm = pl.BlockSpec(memory_space=pl.ANY)
    dma = pltpu.SemaphoreType.DMA
    return pl.pallas_call(
        kernel,
        out_shape=(
            jax.ShapeDtypeStruct((1, 1, SLOTS, FF), BF16),
            jax.ShapeDtypeStruct((1, WIDTH, FF), F32),
        ),
        in_specs=[hbm, vmem, vmem, hbm, hbm],
        out_specs=(vmem, vmem),
        scratch_shapes=[
            pltpu.VMEM((NZ * TOK, NX * WIDTH), BF16),
            pltpu.VMEM((NSB, GROUPS, PART, WMAX), BF16),
            pltpu.VMEM((SLOTS, NX * WIDTH), BF16),
            pltpu.VMEM((NX, SLOTS, FF), BF16),
            pltpu.VMEM((SLOTS, FF), BF16),
            pltpu.VMEM((WIDTH, FF), BF16),
            pltpu.VMEM((SLOTS, FF), F32),
            pltpu.VMEM((3, SLOTS, FF), BF16),
            pltpu.VMEM((2, HALF, FF), BF16),
            pltpu.VMEM((2, SLOTS, FF), BF16),
            pltpu.VMEM((NX, NZ, GROUPS, TOK), F32),
            pltpu.VMEM((NX, NZ, GROUPS, TOK), F32),
            pltpu.VMEM((NX, NZ, GROUPS, TOK), I32),
            dma((2 + NK,)),
            dma((NK,)), dma((NK,)),
            dma((NX,)), dma((NX,)),
            dma((NZ,)), dma((NZ,)),
            dma((NK * 8,)), dma((NK * 8,)),
            dma((NK * GROUPS,)), dma((NK * GROUPS,)),
            dma((4,)), dma((4,)),
            dma((4,)), dma((4,)),
        ],
        compiler_params=pltpu.CompilerParams(
            collective_id=0, has_side_effects=True, vmem_limit_bytes=62 * 2**20
        ),
        name="expert_backward",
    )(d_out, ids_t, gate_t, saved_hidden, down_weight)


def solution(mesh):
    return jax.shard_map(
        body,
        mesh=mesh,
        in_specs=(
            P("dp", ("ctx", "exp"), None),
            P("dp", ("ctx", "exp"), None),
            P("dp", ("ctx", "exp"), None),
            P("dp", ("ctx", "exp"), None, None),
            P(("ctx", "exp"), "dp", None),
        ),
        out_specs=(P("dp", ("ctx", "exp"), None, None), P(("ctx", "exp"), "dp", None)),
        check_vma=False,
    )
```

```python
import functools

import jax
import jax.numpy as jnp
from jax import lax
from jax.experimental import pallas as pl
from jax.experimental.pallas import tpu as pltpu
from jax.sharding import PartitionSpec as P

MESH = pl.DeviceIdType.MESH
F32, BF16, I32 = jnp.float32, jnp.bfloat16, jnp.int32

NX, NY, NZ, NC = 4, 4, 8, 2
TOK, CAP, FF = 128, 14, 768
GROUPS = NY * NC
PART = NZ * CAP
SLOTS = GROUPS * PART
WIDTH = 1280
HALF = SLOTS // 2
TILE = 128

CHUNKS = (
    (2, 0, 256),
    (2, 256, 384),
    (2, 640, 640),
    (1, 0, 640),
    (1, 640, 640),
    (3, 0, 640),
    (3, 640, 640),
    (0, 0, 640),
    (0, 640, 384),
    (0, 1024, 256),
)
NK = len(CHUNKS)
COL = [sum(c[2] for c in CHUNKS[:k]) for k in range(NK)]
WMAX = max(c[2] for c in CHUNKS)
NSB = 3
LAST = NZ // 2
MAIN_LAG = 7
HIDDEN_AT, PASS_AT = 3, 8
FEATURES_AT = {0: (1, 2), 1: (3, 4), 2: (5, 6)}


def kernel(
    d_out, ids_t, gate_t, hidden, weight, dh_out, wg_out,
    rows, sendbuf, routed, hid, raw, wts, acc, part, part2, partr,
    meta, plane, target,
    loc_sem, xs, xr, ms, mr, gs, gr, rs, rr, ys, yr, hs, hr, ps, pr,
):
    i = lax.axis_index("dp")
    ctx = lax.axis_index("ctx")
    y = lax.axis_index("exp")
    z = ctx // NC
    c = lax.rem(ctx, NC)

    def dev(dx=0, dz=0, dc=0, dy=0):
        return (
            lax.rem(i + dx, NX),
            lax.rem(z + dz, NZ) * NC + lax.rem(c + dc, NC),
            lax.rem(y + dy, NY),
        )

    def remote(src, dst, send, recv, to):
        return pltpu.make_async_remote_copy(
            src_ref=src, dst_ref=dst, send_sem=send, recv_sem=recv, device_id=to, device_id_type=MESH
        )

    load_hidden = pltpu.make_async_copy(hidden.at[0, 0], raw, loc_sem.at[0])
    load_hidden.start()
    load_weight = pltpu.make_async_copy(weight.at[0], wts, loc_sem.at[1])
    load_weight.start()
    own = {}
    for k, (o, first, w) in enumerate(CHUNKS):
        if o == 0:
            start = pl.multiple_of(i * WIDTH + first, 128)
            own[k] = pltpu.make_async_copy(
                d_out.at[0, :, pl.ds(start, w)], rows.at[0:TOK, COL[k] : COL[k] + w], loc_sem.at[2 + k]
            )
            own[k].start()

    barrier = pltpu.get_barrier_semaphore()
    peers = [dict(dx=a) for a in range(1, NX)] + [dict(dz=a) for a in range(1, NZ)]
    peers += [dict(dc=j // NY, dy=j % NY) for j in range(1, GROUPS)]
    for p in peers:
        pl.semaphore_signal(barrier, inc=1, device_id=dev(**p), device_id_type=MESH)

    r = lax.broadcasted_iota(I32, (NZ * GROUPS, TOK), 0)
    dz, dc, dy = r // GROUPS, (r // NY) % NC, r % NY
    expert = ((z + dz) % NZ) * GROUPS + ((c + dc) % NC) * NY + (y + dy) % NY
    gates = jnp.zeros((NZ * GROUPS, TOK), F32)
    for k in range(ids_t.shape[0]):
        gates += jnp.where(ids_t[k : k + 1, :] == expert, gate_t[k : k + 1, :], 0.0)
    meta[0] = gates.reshape(NZ, GROUPS, TOK)

    pl.semaphore_wait(barrier, len(peers))

    xcopy = {}

    def send_features(k):
        o, first, w = CHUNKS[k]
        start = pl.multiple_of(lax.rem(i + NX - o, NX) * WIDTH + first, 128)
        xcopy[k] = remote(
            d_out.at[0, :, pl.ds(start, w)], rows.at[0:TOK, COL[k] : COL[k] + w],
            xs.at[k], xr.at[k], dev(dx=NX - o),
        )
        xcopy[k].start()

    send_features(0)
    mcopy = {}
    for o in range(1, NX):
        mcopy[o] = remote(meta.at[0], meta.at[o], ms.at[o], mr.at[o], dev(dx=NX - o))
        mcopy[o].start()

    ring_copies = []

    def ring_copy(k, way, hop):
        lo, hi = COL[k], COL[k] + CHUNKS[k][2]
        if way == 0:
            src, dst, to = (NZ + 1 - hop) % NZ, NZ - hop, dev(dz=1)
        else:
            src, dst, to = hop - 1, hop, dev(dz=NZ - 1)
        first, n = 0, TOK
        if hop == LAST:
            first, n = way * (TOK // 2), TOK // 2
        src, dst = src * TOK + first, dst * TOK + first
        sem = (k * 2 + way) * LAST + hop - 1
        return remote(rows.at[src : src + n, lo:hi], rows.at[dst : dst + n, lo:hi], rs.at[sem], rr.at[sem], to)

    def ring(k, hop):
        if hop == 0:
            if k in own:
                own[k].wait()
            else:
                xcopy[k].wait_recv()
        for way in range(2):
            if hop > 0:
                ring_copy(k, way, hop).wait_recv()
            if hop < LAST:
                copy = ring_copy(k, way, hop + 1)
                copy.start()
                ring_copies.append(copy)

    gcopy = []

    def send_gates():
        for o in range(1, NX):
            mcopy[o].wait_recv()
        for d in range(1, NZ):
            copy = remote(meta.at[:, d], plane.at[:, NZ - d], gs.at[d], gr.at[d], dev(dz=d))
            copy.start()
            gcopy.append(copy)
        plane[:, 0] = meta[:, 0]

    def make_targets():
        for copy in gcopy:
            copy.wait_recv()
        a = lax.broadcasted_iota(I32, (TOK, TOK), 0)
        b = lax.broadcasted_iota(I32, (TOK, TOK), 1)
        earlier = jnp.where(a < b, 1.0, 0.0).astype(BF16)
        n = NZ * GROUPS
        base = CAP * (lax.broadcasted_iota(I32, (n, TOK), 0) // GROUPS)
        for o in range(NX):
            chosen = plane[o].reshape(n, TOK) != 0.0
            position = jnp.dot(jnp.where(chosen, 1.0, 0.0).astype(BF16), earlier, preferred_element_type=F32)
            target[o] = jnp.where(chosen, position.astype(I32) + base, -1).reshape(NZ, GROUPS, TOK)

    ycopies = {}

    def ycopy(k, j):
        lo, w = COL[k], CHUNKS[k][2]
        dc, dy = j // NY, lax.rem(j, NY)
        group = dc * NY + lax.rem(NY - dy, NY)
        n = k * GROUPS + j
        return remote(
            sendbuf.at[k % NSB, j, :, 0:w],
            routed.at[pl.ds(pl.multiple_of(group * PART, 16), PART), lo : lo + w],
            ys.at[n], yr.at[n], dev(dc=dc, dy=dy),
        )

    def select(k):
        o, _, w = CHUNKS[k]
        lo = COL[k]
        if k >= NSB:
            for j in range(1, GROUPS):
                ycopy(k - NSB, j).wait_send()
        slot = lax.broadcasted_iota(I32, (PART, TOK), 0)

        def picked(j):
            hits, gate = [], jnp.zeros((PART, TOK), F32)
            for d in range(NZ):
                hit = slot == target[o, d, pl.ds(j, 1), :]
                hits.append(jnp.where(hit, 1.0, 0.0).astype(BF16))
                gate += jnp.where(hit, plane[o, d, pl.ds(j, 1), :], 0.0)
            gate = jnp.sum(gate, axis=1, keepdims=True)
            chosen = jnp.dot(
                jnp.concatenate(hits, axis=1), rows[:, lo : lo + w], preferred_element_type=F32
            )
            return (chosen * gate).astype(BF16)

        def one(j, _):
            sendbuf[k % NSB, j, :, 0:w] = picked(j)
            ycopy(k, j).start()
            return 0

        lax.fori_loop(1, GROUPS, one, 0)
        routed[0:PART, lo : lo + w] = picked(0)

    def arrived(k):
        for j in range(1, GROUPS):
            ycopy(k, j).wait_recv()

    def hidden_product(k, fresh):
        _, first, w = CHUNKS[k]
        lo = COL[k]

        def one(t, _):
            at = pl.ds(pl.multiple_of(t * TILE, TILE), TILE)
            got = jnp.dot(routed[at, lo : lo + w], wts[first : first + w, :], preferred_element_type=F32)
            acc[at, :] = got if fresh else acc[at, :] + got
            return 0

        lax.fori_loop(0, SLOTS // TILE, one, 0)

    def weight_product(k):
        o, first, w = CHUNKS[k]
        lo = COL[k]

        def one(t, _):
            got = lax.dot_general(
                routed[:, pl.ds(pl.multiple_of(lo + t * TILE, TILE), TILE)], hid[o],
                (((0,), (0,)), ((), ())), preferred_element_type=F32,
            )
            at = pl.ds(pl.multiple_of(first + t * TILE, TILE), TILE)
            wg_out[0, at, :] += got
            return 0

        lax.fori_loop(0, w // TILE, one, 0)

    def origin(n):
        block = ((n.astype(F32) + 0.5) * (1.0 / CAP)).astype(I32)
        slot = n - block * CAP
        group = ((block.astype(F32) + 0.5) * (1.0 / NZ)).astype(I32)
        d = block - group * NZ
        dc = jnp.where(group >= NY, 1, 0)
        dy = group - dc * NY
        dz = z + d
        dz = jnp.where(dz >= NZ, dz - NZ, dz)
        dy = y + dy
        dy = jnp.where(dy >= NY, dy - NY, dy)
        dc = c + dc
        dc = jnp.where(dc >= NC, dc - NC, dc)
        return CAP * (dz * GROUPS + dc * NY + dy) + slot

    hcopy = {}

    def send_hidden():
        load_hidden.wait()

        def one(t, _):
            n = lax.broadcasted_iota(I32, (TILE, 1), 0) + t * TILE
            m = lax.broadcasted_iota(I32, (TILE, SLOTS), 1)
            pick = jnp.where(origin(n) == m, 1.0, 0.0).astype(BF16)
            at = pl.ds(pl.multiple_of(t * TILE, TILE), TILE)
            hid[0, at, :] = jnp.dot(pick, raw[...], preferred_element_type=F32).astype(BF16)
            return 0

        lax.fori_loop(0, SLOTS // TILE, one, 0)
        hcopy[0] = remote(hid.at[0], hid.at[3], hs.at[0], hr.at[0], dev(dx=1))
        hcopy[1] = remote(hid.at[0], hid.at[1], hs.at[1], hr.at[1], dev(dx=NX - 1))
        hcopy[0].start()
        hcopy[1].start()

    def pass_hidden():
        hcopy[0].wait_recv()
        hcopy[2] = remote(hid.at[3, 0:HALF], hid.at[2, 0:HALF], hs.at[2], hr.at[2], dev(dx=1))
        hcopy[2].start()
        hcopy[1].wait_recv()
        hcopy[3] = remote(hid.at[1, HALF:SLOTS], hid.at[2, HALF:SLOTS], hs.at[3], hr.at[3], dev(dx=NX - 1))
        hcopy[3].start()

    def got_far_hidden():
        hcopy[2].wait_recv()
        hcopy[3].wait_recv()

    pcopy = {}

    def send_far():
        part[1] = acc[...].astype(BF16)
        pcopy[0] = remote(part.at[1, 0:HALF], part2.at[0], ps.at[0], pr.at[0], dev(dx=1))
        pcopy[1] = remote(part.at[1, HALF:SLOTS], part2.at[1], ps.at[1], pr.at[1], dev(dx=NX - 1))
        pcopy[0].start()
        pcopy[1].start()

    def send_near(way):
        pcopy[way].wait_recv()
        if way == 0:
            part[0, 0:HALF] = (acc[0:HALF] + part2[0].astype(F32)).astype(BF16)
            part[0, HALF:SLOTS] = acc[HALF:SLOTS].astype(BF16)
            pcopy[2] = remote(part.at[0], partr.at[0], ps.at[2], pr.at[2], dev(dx=1))
            pcopy[2].start()
        else:
            part[2, 0:HALF] = acc[0:HALF].astype(BF16)
            part[2, HALF:SLOTS] = (acc[HALF:SLOTS] + part2[1].astype(F32)).astype(BF16)
            pcopy[3] = remote(part.at[2], partr.at[1], ps.at[3], pr.at[3], dev(dx=NX - 1))
            pcopy[3].start()

    def finish():
        pcopy[2].wait_recv()
        pcopy[3].wait_recv()
        total = acc[...] + partr[0].astype(F32) + partr[1].astype(F32)
        part[1] = total.astype(BF16)

        def one(t, _):
            n = lax.broadcasted_iota(I32, (1, SLOTS), 1)
            m = lax.broadcasted_iota(I32, (TILE, SLOTS), 0) + t * TILE
            pick = jnp.where(origin(n) == m, 1.0, 0.0).astype(BF16)
            at = pl.ds(pl.multiple_of(t * TILE, TILE), TILE)
            dh_out[0, 0, at, :] = jnp.dot(pick, part[1], preferred_element_type=F32).astype(BF16)
            return 0

        lax.fori_loop(0, SLOTS // TILE, one, 0)

    def main(k):
        o, first, w = CHUNKS[k]
        arrived(k)
        if k == 0:
            load_weight.wait()
        hidden_product(k, first == 0)
        if first + w == WIDTH:
            if o == 2:
                send_far()
            elif o == 1:
                send_near(0)
            elif o == 3:
                send_near(1)
                pcopy[0].wait_send()
                pcopy[1].wait_send()
        if o != 2:
            weight_product(k)
        if (o, first) == (3, 0):
            got_far_hidden()
        if o == 3:
            for m in range(NK):
                if CHUNKS[m][0] == 2 and (CHUNKS[m][1] < WIDTH // 2) == (first == 0):
                    weight_product(m)

    for q in range(2 * NK + MAIN_LAG):
        for k in reversed(range(NK)):
            if 0 <= q - 2 * k <= LAST:
                ring(k, q - 2 * k)
        for k in FEATURES_AT.get(q, ()):
            send_features(k)
        if q == 0:
            send_gates()
        if q == 1:
            for first in range(0, WIDTH, TILE):
                wg_out[0, first : first + TILE, :] = jnp.zeros((TILE, FF), F32)
        if q == 2:
            make_targets()
        if q == HIDDEN_AT:
            send_hidden()
        if q == PASS_AT:
            pass_hidden()
        k, odd = divmod(q - LAST, 2)
        if 0 <= k < NK and not odd:
            select(k)
        k, odd = divmod(q - MAIN_LAG, 2)
        if 0 <= k < NK and not odd:
            main(k)
    finish()

    for o in range(1, NX):
        mcopy[o].wait_send()
    for k in xcopy:
        xcopy[k].wait_send()
    for copy in gcopy + ring_copies:
        copy.wait_send()
    for k in range(max(0, NK - NSB), NK):
        for j in range(1, GROUPS):
            ycopy(k, j).wait_send()
    for n in range(4):
        hcopy[n].wait_send()
    pcopy[2].wait_send()
    pcopy[3].wait_send()


def body(d_out, route_ids, gate_weights, saved_hidden, down_weight):
    ids_t = route_ids[0].T
    gate_t = gate_weights[0].T
    vmem = pl.BlockSpec(memory_space=pltpu.VMEM)
    hbm = pl.BlockSpec(memory_space=pl.ANY)
    dma = pltpu.SemaphoreType.DMA
    return pl.pallas_call(
        kernel,
        out_shape=(
            jax.ShapeDtypeStruct((1, 1, SLOTS, FF), BF16),
            jax.ShapeDtypeStruct((1, WIDTH, FF), F32),
        ),
        in_specs=[hbm, vmem, vmem, hbm, hbm],
        out_specs=(vmem, vmem),
        scratch_shapes=[
            pltpu.VMEM((NZ * TOK, NX * WIDTH), BF16),
            pltpu.VMEM((NSB, GROUPS, PART, WMAX), BF16),
            pltpu.VMEM((SLOTS, NX * WIDTH), BF16),
            pltpu.VMEM((NX, SLOTS, FF), BF16),
            pltpu.VMEM((SLOTS, FF), BF16),
            pltpu.VMEM((WIDTH, FF), BF16),
            pltpu.VMEM((SLOTS, FF), F32),
            pltpu.VMEM((3, SLOTS, FF), BF16),
            pltpu.VMEM((2, HALF, FF), BF16),
            pltpu.VMEM((2, SLOTS, FF), BF16),
            pltpu.VMEM((NX, NZ, GROUPS, TOK), F32),
            pltpu.VMEM((NX, NZ, GROUPS, TOK), F32),
            pltpu.VMEM((NX, NZ, GROUPS, TOK), I32),
            dma((2 + NK,)),
            dma((NK,)), dma((NK,)),
            dma((NX,)), dma((NX,)),
            dma((NZ,)), dma((NZ,)),
            dma((NK * 8,)), dma((NK * 8,)),
            dma((NK * GROUPS,)), dma((NK * GROUPS,)),
            dma((4,)), dma((4,)),
            dma((4,)), dma((4,)),
        ],
        compiler_params=pltpu.CompilerParams(
            collective_id=0, has_side_effects=True, vmem_limit_bytes=62 * 2**20
        ),
        name="expert_backward",
    )(d_out, ids_t, gate_t, saved_hidden, down_weight)


def solution(mesh):
    return jax.shard_map(
        body,
        mesh=mesh,
        in_specs=(
            P("dp", ("ctx", "exp"), None),
            P("dp", ("ctx", "exp"), None),
            P("dp", ("ctx", "exp"), None),
            P("dp", ("ctx", "exp"), None, None),
            P(("ctx", "exp"), "dp", None),
        ),
        out_specs=(P("dp", ("ctx", "exp"), None, None), P(("ctx", "exp"), "dp", None)),
        check_vma=False,
    )
```
